512 devices in a mesh: lat: 16 (over y_hi, z), lon: 32 (over y_lo, x, core).
Axes of the slice: x: 4, y: 8 (y_hi: 2, y_lo: 4; y = y_hi * 4 + y_lo), z: 8, core: 2. Of those that a mesh axis runs over, the one named last changes fastest.
Arguments:
- grad_out: float32 [160, 720, 1440], P('lon', 'lat'), may hold values from -6 to 6
- saved_spectra: float32 [720, 96, 2, 160], P('lat', 'lon'), may hold values from -0.4375 to 0.4375
- spec_weight: float32 [720, 2, 160], replicated, may hold values from -6 to 6
- legendre: float32 [96, 720, 720], P('lon', 'lat'), may hold values from -0.3125 to 0.3125
- lat_weight: float32 [720], P('lat'), may hold values from 0.25 to 1.75
Outputs:
- grad_in: float32 [160, 720, 1440], P('lon', 'lat')
- grad_weight: float32 [720, 2, 160], P('lat')
The draws below stay inside these ranges and needn't reach their ends.
All inputs are finite; a program needn't handle non-finite values.
Results may differ from the reference program's by a relative error of at most 0.000071.
Values sent between devices are 32-bit elements; how exact they have to be, the bound alone decides.
No kernel may reach another device: no remote copies, remote signals or barrier semaphores. Data moves between devices by JAX's collectives and lax.ppermute only.
A program may use at most 64 MiB of HBM per device.

```python
import math
import jax
import jax.numpy as jnp
from jax import lax

CHANNELS = 160
NLAT = 720
NLON = 1440
DEGREES = 720
ORDERS = 96


def with_spikes(array, own_key, source, target, blocks, factor):
    def block_of(axis_at):
        return (jnp.arange(array.shape[axis_at]) // (array.shape[axis_at] // blocks)).reshape((-1,) + (1,) * (array.ndim - 1 - axis_at))

    near = jax.random.permutation(own_key, blocks)[block_of(target)]
    far = (block_of(target) + blocks // 2) % blocks
    return jnp.where((block_of(source) == near) | (block_of(source) == far), factor * array, array)


def block_scale(own_key, extent, shards, low, high):
    def one(dim, parts):
        draws = jax.random.uniform(jax.random.fold_in(jax.random.fold_in(own_key, 6), dim), (parts,), jnp.float32, low / len(shards), high / len(shards))
        return jnp.repeat(jnp.exp(draws), extent[dim] // parts).reshape((-1,) + (1,) * (len(extent) - dim - 1))

    loudness = one(*shards[0])
    for cut in shards[1:]:
        loudness = loudness * one(*cut)
    return loudness


def noise(stream_key, dims, width, most, shards=(), kind=jnp.bfloat16):
    factor_of = block_scale(stream_key, dims, shards, -0.22, 0.18) if shards else 1.0
    entries = jax.random.normal(stream_key, dims, jnp.float32) * width * factor_of
    return jnp.minimum(jnp.maximum(entries, -most), most).astype(kind)


def noise_with(own_key, dims, deviation, most, shards, heavy, kind=jnp.bfloat16):
    entries = deviation * jax.random.normal(own_key, dims, jnp.float32)
    if shards:
        entries = entries * block_scale(own_key, dims, shards, -0.22, 0.18)
    return jnp.clip(with_spikes(entries, jax.random.fold_in(own_key, 3), *heavy), -most, most).astype(kind)


def setup_inputs(seed: int = 0) -> dict:
    key_of = jax.random.split(jax.random.key(seed), 6)
    grad_out = noise(key_of[0], (CHANNELS, NLAT, NLON), 1.0, 6.0, ((0, 32), (1, 16)), jnp.float32)
    saved_spectra = noise(key_of[1], (DEGREES, ORDERS, 2, CHANNELS), ((2 * ORDERS) ** -0.5), 0.4375, ((0, 16), (1, 32)), jnp.float32)
    spec_weight = noise(key_of[2], (DEGREES, 2, CHANNELS), 1.0, 6.0, (), jnp.float32)
    legendre = noise_with(key_of[3], (ORDERS, NLAT, DEGREES), NLAT ** -0.5, 0.3125, ((0, 32), (1, 16)), (1, 2, 16, 2.0), jnp.float32)
    lat_weight = jnp.clip(0.25 + 1.5 * jax.random.uniform(key_of[4], (NLAT,), jnp.float32) ** block_scale(key_of[4], (NLAT,), ((0, 16),), -0.2, 0.2), 0.25, 1.75)
    return dict(grad_out=grad_out, saved_spectra=saved_spectra, spec_weight=spec_weight, legendre=legendre, lat_weight=lat_weight)


def wave_tables(orders, points):
    order_ids = jnp.arange(orders, dtype=jnp.int32)
    point_ids = jnp.arange(points, dtype=jnp.int32)
    phase = order_ids[:, None] * point_ids[None, :] % points
    angle_grid = 2.0 * math.pi / points * phase.astype(jnp.float32)
    return (jnp.cos(angle_grid), jnp.sin(angle_grid))

def conj_times(first, second):
    real_first = first[..., 0, :]
    imag_first = first[..., 1, :]
    real_second = second[..., 0, :]
    imag_second = second[..., 1, :]
    real_part = real_first * real_second + imag_first * imag_second
    imag_part = real_first * imag_second - imag_first * real_second
    return jnp.stack([real_part, imag_part], axis=-2)

def reference(grad_out, saved_spectra, spec_weight, legendre, lat_weight):
    cosine, sine = wave_tables(ORDERS, NLON)
    norm_factor = 1.0 / math.sqrt(NLON)
    forward_table = jnp.concatenate([cosine, -sine], axis=0).T * norm_factor
    rows_all = grad_out.reshape(CHANNELS * NLAT, NLON)
    coeffs = jnp.dot(rows_all, forward_table, precision=lax.Precision.HIGHEST, preferred_element_type=jnp.float32).reshape(CHANNELS, NLAT, 2, ORDERS)
    spectra = jnp.einsum('mpl,cprm->lmrc', legendre, coeffs, precision=lax.Precision.HIGHEST)
    grad_weight = lax.optimization_barrier(jnp.sum(conj_times(saved_spectra, spectra), axis=1))
    adjoint = conj_times(spec_weight[:, None], spectra)
    synthesis = jnp.einsum('mpl,lmrc->cprm', legendre, adjoint, precision=lax.Precision.HIGHEST)
    synthesis = synthesis * lat_weight[None, :, None, None]
    order_ids = jnp.arange(ORDERS, dtype=jnp.int32)
    doubling = jnp.where(order_ids == 0, 1.0, 2.0).astype(jnp.float32)
    inverse_table = jnp.concatenate([cosine * doubling[:, None], -sine * doubling[:, None]], axis=0) * norm_factor
    grad_in = jnp.dot(synthesis.reshape(CHANNELS * NLAT, 2 * ORDERS), inverse_table, precision=lax.Precision.HIGHEST, preferred_element_type=jnp.float32)
    return (grad_in.reshape(CHANNELS, NLAT, NLON), grad_weight)
```

```python
import math

import jax
import jax.numpy as jnp
import numpy as np
from jax import lax
from jax.sharding import Mesh, PartitionSpec as P

NAMES = ("yh", "z", "yl", "xh", "xl", "c")
SIZES = (2, 8, 4, 2, 2, 2)
LAT = ("yh", "z")
LON = ("yl", "xh", "xl", "c")
GROUP = ("yh", "z", "yl", "xh")
HIGH = lax.Precision.HIGH
EXACT = lax.Precision.HIGHEST


def order_of(yh, z, yl, xh, xl):
    xl_o = np.where(z < 3, xl, 1 - xl)
    m = 3 * (((yl * 2 + xh) * 2 + xl_o) * 2 + yh) + z % 3
    return np.where(z < 6, m, -1)


def tables(points):
    yh, z, yl, xh = np.meshgrid(*[np.arange(n) for n in SIZES[:4]], indexing="ij")
    out = []
    for xl in range(2):
        m = order_of(yh, z, yl, xh, xl).reshape(-1)
        phase = (m[:, None] * np.arange(points)[None]) % points
        angle = 2.0 * math.pi / points * phase
        rows = np.stack([np.cos(angle), -np.sin(angle)]) / math.sqrt(points)
        out.append(np.where(m[None, :, None] >= 0, rows, 0.0))
    return np.stack(out).astype(np.float32)


def channel_picks(channels):
    per = channels // 32
    picks = np.zeros((2, channels, channels), np.float32)
    for xl in range(2):
        slot = 0
        for region in (xl, 1 - xl):
            for c in range(2):
                for yl in range(4):
                    for xh in range(2):
                        for j in range(per):
                            b = ((yl * 2 + xh) * 2 + region) * 2 + c
                            picks[xl, b * per + j, slot] = 1.0
                            slot += 1
    return picks


def local(grad_out, saved_spectra, spec_weight, legendre, lat_weight):
    group, rows, points = grad_out.shape
    degrees, _, channels = spec_weight.shape
    orders = legendre.shape[0]
    pad = -rows % 8
    wide = rows + pad
    xl, c = lax.axis_index("xl"), lax.axis_index("c")
    half, quarter = channels // 2, channels // 4

    picks = jnp.asarray(channel_picks(channels))[xl]
    sv = jnp.dot(saved_spectra.reshape(-1, channels), picks, precision=EXACT)
    sv = sv.reshape(rows, orders, 2, 2, half).transpose(3, 1, 0, 2, 4).reshape(2, orders, rows, 2 * half)
    own = jnp.concatenate([legendre, sv[0]], axis=-1)
    other = jnp.concatenate([legendre, sv[1]], axis=-1)
    own = lax.ppermute(own, ("yh", "c"), [(a * 2 + b, b * 2 + a) for a in range(2) for b in range(2)])
    other = lax.ppermute(
        other,
        ("yh", "xl", "c"),
        [(a * 4 + x * 2 + b, b * 4 + (1 - x) * 2 + a) for a in range(2) for x in range(2) for b in range(2)],
    )

    table = jnp.asarray(tables(points))[xl]
    field = jnp.pad(grad_out, ((0, 0), (0, pad), (0, 0))).reshape(group * wide, points)
    coeffs = jnp.einsum("rmx,qx->mrq", table, field, precision=HIGH)
    coeffs = jnp.pad(coeffs.reshape(128, 2 * group * wide), ((0, 0), (0, 512 - 2 * group * wide)))
    coeffs = lax.all_to_all(coeffs.reshape(128, 4, 128), GROUP, 0, 0, tiled=True)

    sent = jnp.concatenate([own, other, own[:2]], axis=0)
    sent, coeffs = lax.optimization_barrier((sent, coeffs))
    got = lax.all_to_all(sent, ("z",), 0, 0, tiled=True)
    got = lax.all_to_all(jnp.stack([got, got]), ("c",), 0, 0, tiled=True)
    got = got.reshape(16, rows, degrees + 2 * half)
    leg = jnp.pad(got[..., :degrees], ((0, 0), (0, pad), (0, 0))).reshape(16 * wide, degrees)
    sv = got[..., degrees:].reshape(degrees, 2, 2, quarter)
    sv = jnp.where(c == 0, sv[:, :, 0], sv[:, :, 1]).transpose(1, 2, 0)

    coeffs = coeffs.reshape(128, 512)[:, : 2 * group * wide].reshape(16, 8, 2, group, wide)
    coeffs = coeffs.transpose(2, 1, 3, 0, 4).reshape(2, quarter, 16 * wide)
    spectra = jnp.einsum("rhp,pl->rhl", coeffs, leg, precision=HIGH)
    weight = jnp.dot(spec_weight.reshape(-1, channels), picks[:, :half], precision=EXACT)
    weight = weight.reshape(degrees, 2, 2, quarter)
    weight = jnp.where(c == 0, weight[:, :, 0], weight[:, :, 1]).transpose(1, 2, 0)

    def conj_times(first, second):
        return jnp.stack(
            [first[0] * second[0] + first[1] * second[1], first[0] * second[1] - first[1] * second[0]]
        )

    yh, z, yl, xh = (lax.axis_index(n) for n in GROUP)
    first = (yl + xh + yh == 0) & (z == 3 * xl)
    twice = jnp.where(first, 1.0, 2.0)
    part = conj_times(sv, spectra)
    adjoint = conj_times(weight, spectra) * twice
    synthesis = jnp.einsum("rhl,pl->rhp", adjoint, leg, precision=HIGH)

    synthesis = synthesis.reshape(2, 8, group, 16, wide)
    part = jnp.pad(part.reshape(2, 8, group, 16, rows), ((0, 0),) * 4 + ((0, pad),))
    back = jnp.stack([synthesis, part]).transpose(4, 2, 0, 1, 3, 5).reshape(128, 4 * group * wide)
    back = jnp.pad(back, ((0, 0), (0, 1024 - 4 * group * wide))).reshape(128, 8, 128)
    back = lax.all_to_all(back, GROUP, 0, 0, tiled=True)
    back = back.reshape(128, 1024)[:, : 4 * group * wide].reshape(128, 2, 2, group * wide)

    share = jnp.sum(back[:, 1], axis=0).reshape(2 * group * wide)
    share = jnp.pad(share, (0, 512 - 2 * group * wide)).reshape(1, 4, 128)
    share = lax.all_to_all(jnp.broadcast_to(share, (32, 4, 128)), LON, 0, 0, tiled=True)
    grad_weight = share.reshape(32, 512)[:, : 2 * group * wide].reshape(32, 2, group, wide)[..., :rows]
    grad_weight = grad_weight.transpose(3, 1, 0, 2).reshape(rows, 2, channels)

    grad_in = jnp.einsum("mrq,rmx->qx", back[:, 0], table, precision=HIGH)
    grad_in = grad_in.reshape(group, wide, points)[:, :rows] * lat_weight[None, :, None]
    return (grad_in, grad_weight)


def solution(mesh):
    fine = Mesh(mesh.devices.reshape(SIZES), NAMES)
    return jax.shard_map(
        local,
        mesh=fine,
        in_specs=(P(LON, LAT, None), P(LAT, LON, None, None), P(), P(LON, LAT, None), P(LAT)),
        out_specs=(P(LON, LAT, None), P(LAT, None, None)),
        check_vma=False,
    )
```

```python
import functools
import math

import jax
import jax.numpy as jnp
import ml_dtypes
import numpy as np
from jax import lax
from jax.experimental import pallas as pl
from jax.experimental.pallas import tpu as pltpu
from jax.sharding import Mesh, PartitionSpec as P

NAMES = ("yh", "z", "yl", "xh", "xl", "c")
SIZES = (2, 8, 4, 2, 2, 2)
LAT = ("yh", "z")
LON = ("yl", "xh", "xl", "c")
GROUP = ("yh", "z", "yl", "xh")
BF = jnp.bfloat16
F32 = jnp.float32
WIDE = 48
NN = (((1,), (0,)), ((), ()))
NT = (((1,), (1,)), ((), ()))
TN = (((0,), (0,)), ((), ()))


def order_of(yh, z, yl, xh, xl):
    xl_o = np.where(z < 3, xl, 1 - xl)
    m = 3 * (((yl * 2 + xh) * 2 + xl_o) * 2 + yh) + z % 3
    return np.where(z < 6, m, -1)


@functools.cache
def tables(points):
    yh, z, yl, xh = np.meshgrid(*[np.arange(n) for n in SIZES[:4]], indexing="ij")
    out = []
    for xl in range(2):
        m = order_of(yh, z, yl, xh, xl).reshape(-1)
        phase = (m[:, None] * np.arange(points)[None]) % points
        angle = 2.0 * math.pi / points * phase
        rows = np.stack([np.cos(angle), -np.sin(angle)]) / math.sqrt(points)
        out.append(np.where(m[None, :, None] >= 0, rows, 0.0).reshape(256, points))
    full = np.stack(out).astype(np.float32)
    high = full.astype(ml_dtypes.bfloat16)
    low = (full - high.astype(np.float32)).astype(ml_dtypes.bfloat16)
    return high, low


@functools.cache
def channel_slots(channels):
    per = channels // 32
    out = []
    for xl in range(2):
        out.append(
            [
                (((yl * 2 + xh) * 2 + region) * 2 + c) * per + j
                for region in (xl, 1 - xl)
                for c in range(2)
                for j in range(per)
                for yl in range(4)
                for xh in range(2)
            ]
        )
    return np.asarray(out, np.int32)


def dot(a, b, dims):
    return lax.dot_general(a, b, dims, preferred_element_type=F32)


def two(x):
    high = x.astype(BF)
    return high, (x - high.astype(F32)).astype(BF)


def three(x):
    high, rest = x.astype(BF), None
    rest = x - high.astype(F32)
    mid = rest.astype(BF)
    return high, mid, (rest - mid.astype(F32)).astype(BF)


def params(flops, nbytes, vmem=48):
    return dict(
        compiler_params=pltpu.CompilerParams(vmem_limit_bytes=vmem * 2**20),
        cost_estimate=pl.CostEstimate(flops=flops, bytes_accessed=nbytes, transcendentals=0),
    )


def prepare_kernel(slots_ref, leg_ref, saved_ref, own_ref, other_ref):
    orders, rows, degrees = leg_ref.shape
    channels = saved_ref.shape[3]
    half = channels // 2
    pick = (lax.broadcasted_iota(jnp.int32, (channels, channels), 0) == slots_ref[...]).astype(F32).astype(BF)
    for k in range(orders):
        for ref in (own_ref, other_ref):
            ref[k, WIDE - 8 : WIDE, :] = jnp.zeros((8, ref.shape[2]), F32)
            ref[k, :rows, :degrees] = leg_ref[k]
            ref[k, :, degrees + channels :] = jnp.zeros((WIDE, ref.shape[2] - degrees - channels), F32)
        for r in range(2):
            v = saved_ref[:, k, r, :]
            out = sum(dot(term, pick, NN) for term in three(v))
            at = degrees + r * half
            own_ref[k, :rows, at : at + half] = out[:, :half]
            other_ref[k, :rows, at : at + half] = out[:, half:]


def weight_kernel(place_ref, slots_ref, w_ref, out_ref):
    degrees, _, channels = w_ref.shape
    quarter = channels // 4
    pick = (lax.broadcasted_iota(jnp.int32, (channels, 2 * quarter), 0) == slots_ref[...]).astype(F32).astype(BF)
    c = place_ref[1]
    for r in range(2):
        out = sum(dot(pick, term, (((0,), (1,)), ((), ()))) for term in three(w_ref[:, r, :]))
        out_ref[r * quarter : (r + 1) * quarter, :] = jnp.where(
            c == 0, out[:quarter], out[quarter : 2 * quarter]
        )


def forward_kernel(place_ref, g_ref, th_ref, tl_ref, out_ref, field):
    group, rows, points = g_ref.shape
    field[...] = jnp.zeros_like(field)
    for j in range(group):
        field[j * WIDE : j * WIDE + rows, :] = g_ref[j]
    high, low = two(field[...])
    table = th_ref[0]
    acc = dot(table, high, NT) + dot(table, low, NT) + dot(tl_ref[0], high, NT)
    for r in range(2):
        for k in range(2):
            out_ref[:, 2 * r + k, :] = acc[r * 128 : (r + 1) * 128, k * 128 : (k + 1) * 128]


def split_kernel(place_ref, near_ref, far_ref, lh_ref, ll_ref, sv_ref, dense):
    blocks, _, _ = near_ref.shape
    degrees = lh_ref.shape[1]
    span = blocks * WIDE
    quarter = sv_ref.shape[0] // 2
    c = place_ref[1]
    for ref, side in ((near_ref, c), (far_ref, 1 - c)):
        at = pl.multiple_of(side * span, span)
        x = ref[...].reshape(span, ref.shape[2])
        high, low = two(x[:, :degrees])
        lh_ref[pl.ds(at, span), :] = high
        ll_ref[pl.ds(at, span), :] = low
        dense[pl.ds(at, span), :] = x[:, degrees - degrees % 128 :]
    turned = dense[...].T
    off = degrees % 128
    for r in range(2):
        first = turned[off + (2 * r) * quarter : off + (2 * r + 1) * quarter]
        second = turned[off + (2 * r + 1) * quarter : off + (2 * r + 2) * quarter]
        mine = jnp.where(c == 0, first, second)
        for a in range(2 * blocks):
            sv_ref[r * quarter : (r + 1) * quarter, a * 45 : a * 45 + 45] = mine[:, a * WIDE : a * WIDE + 45]


def core_kernel(place_ref, x_ref, lh_ref, ll_ref, sv_ref, w_ref, out_ref, ct, tmp, back):
    group, bands = 5, 16
    quarter = sv_ref.shape[0] // 2
    rows = 45
    back[...] = jnp.zeros_like(back)
    for k in range(4):
        tmp[:, k * 128 : (k + 1) * 128] = x_ref[:, k, :]
    for a in range(bands):
        for r in range(2):
            for j in range(group):
                q = (r * group + j) * 8
                lane = r * 256 + j * WIDE
                ct[q : q + 8, a * WIDE : (a + 1) * WIDE] = tmp[a * 8 : a * 8 + 8, lane : lane + WIDE]
    ch, cl = two(ct[...])
    n = 2 * quarter
    both = dot(jnp.concatenate([ch, cl], axis=0), lh_ref[...], NN)
    spec = both[:n] + both[n:] + dot(ch, ll_ref[...], NN)
    g, h = spec[:quarter], spec[quarter:]
    u, v = w_ref[:quarter, :], w_ref[quarter:, :]
    twice = jnp.where(place_ref[2] == 1, 1.0, 2.0).astype(F32)
    adjoint = jnp.concatenate([(u * g + v * h) * twice, (u * h - v * g) * twice], axis=0)
    p, q = sv_ref[:quarter, :], sv_ref[quarter:, :]
    part = (p * g + q * h, p * h - q * g)
    ah, al = two(adjoint)
    both = dot(jnp.concatenate([ah, al], axis=0), lh_ref[...], NT)
    syn = both[:n] + both[n:] + dot(ah, ll_ref[...], NT)
    for a in range(bands):
        for r in range(2):
            for j in range(group):
                at = (r * group + j) * 8
                lane = r * 256 + j * WIDE
                back[a * 8 : a * 8 + 8, lane : lane + WIDE] = syn[at : at + 8, a * WIDE : (a + 1) * WIDE]
                back[a * 8 : a * 8 + 8, 512 + lane : 512 + lane + rows] = part[r][
                    j * 8 : j * 8 + 8, a * rows : (a + 1) * rows
                ]
    for k in range(8):
        out_ref[:, k, :] = back[:, k * 128 : (k + 1) * 128]


def share_kernel(x_ref, out_ref):
    total = jnp.sum(x_ref[...], axis=0)[4:8]
    out_ref[...] = jnp.broadcast_to(total[None], out_ref.shape)


def inverse_kernel(place_ref, x_ref, th_ref, tl_ref, lw_ref, out_ref):
    group, rows, points = out_ref.shape
    block = jnp.concatenate(
        [jnp.concatenate([x_ref[:, 2 * r, :], x_ref[:, 2 * r + 1, :]], axis=1) for r in range(2)], axis=0
    )
    high, low = two(block)
    table = th_ref[0]
    acc = dot(high, table, TN) + dot(low, table, TN) + dot(high, tl_ref[0], TN)
    for j in range(group):
        out_ref[j] = acc[j * WIDE : j * WIDE + rows] * lw_ref[...]


def whole(shape):
    return pl.BlockSpec(shape, lambda i, place: (0,) * len(shape))


def call(kernel, place, args, out_shapes, scratch=(), picked=(), **extra):
    specs = []
    for i, a in enumerate(args):
        if i in picked:
            specs.append(pl.BlockSpec((1, *a.shape[1:]), lambda _, p, n=a.ndim: (p[0],) + (0,) * (n - 1)))
        else:
            specs.append(whole(a.shape))
    return pl.pallas_call(
        kernel,
        out_shape=out_shapes,
        grid_spec=pltpu.PrefetchScalarGridSpec(
            num_scalar_prefetch=1,
            grid=(1,),
            in_specs=specs,
            out_specs=jax.tree.map(lambda s: whole(s.shape), out_shapes),
            scratch_shapes=list(scratch),
        ),
        **extra,
    )(place, *args)


def drop_place(kernel):
    return lambda place_ref, *refs: kernel(*refs)


def shape(*dims, dtype=F32):
    return jax.ShapeDtypeStruct(dims, dtype)


def local(grad_out, saved_spectra, spec_weight, legendre, lat_weight):
    group, rows, points = grad_out.shape
    degrees, _, channels = spec_weight.shape
    orders = legendre.shape[0]
    lanes = -(-(degrees + channels) // 128) * 128
    half, quarter = channels // 2, channels // 4
    yh, z, yl, xh, xl, c = (lax.axis_index(n) for n in NAMES)
    first = (yl + xh + yh == 0) & (z == 3 * xl)
    place = jnp.stack([xl, c, first.astype(jnp.int32)]).astype(jnp.int32)
    slot_table = jnp.asarray(channel_slots(channels))
    slots = jnp.where(xl == 0, slot_table[0:1], slot_table[1:2])
    high, low = (jnp.asarray(t) for t in tables(points))

    own, other = call(
        drop_place(prepare_kernel),
        place,
        (slots, legendre, saved_spectra),
        (shape(orders, WIDE, lanes), shape(orders, WIDE, lanes)),
        **params(60_000_000, 4_000_000),
    )
    own = lax.ppermute(own, ("yh", "c"), [(a * 2 + b, b * 2 + a) for a in range(2) for b in range(2)])
    other = lax.ppermute(
        other,
        ("yh", "xl", "c"),
        [(a * 4 + x * 2 + b, b * 4 + (1 - x) * 2 + a) for a in range(2) for x in range(2) for b in range(2)],
    )
    sent = jnp.concatenate([own, other, own[:2]], axis=0)
    near = lax.all_to_all(sent, ("z",), 0, 0, tiled=True)
    far = lax.ppermute(near, ("c",), [(0, 1), (1, 0)])

    coeffs = call(
        forward_kernel,
        place,
        (grad_out, high, low),
        shape(128, 4, 128),
        scratch=[pltpu.VMEM((256, points), F32)],
        picked=(1, 2),
        **params(600_000_000, 3_000_000),
    )
    weight = call(
        weight_kernel, place, (slots[:, :half], spec_weight), shape(2 * quarter, degrees),
        **params(200_000_000, 2_000_000),
    )
    coeffs, near_done = lax.optimization_barrier((coeffs, near))
    coeffs = lax.all_to_all(coeffs, GROUP, 0, 0, tiled=True)
    leg_high, leg_low, sv = call(
        split_kernel,
        place,
        (near_done, far),
        (
            shape(16 * WIDE, degrees, dtype=BF),
            shape(16 * WIDE, degrees, dtype=BF),
            shape(2 * quarter, degrees),
        ),
        scratch=[pltpu.VMEM((16 * WIDE, lanes - degrees + degrees % 128), F32)],
        **params(100_000_000, 6_000_000),
    )
    back = call(
        core_kernel,
        place,
        (coeffs, leg_high, leg_low, sv, weight),
        shape(128, 8, 128),
        scratch=[
            pltpu.VMEM((2 * quarter, 16 * WIDE), F32),
            pltpu.VMEM((128, 512), F32),
            pltpu.VMEM((128, 1024), F32),
        ],
        **params(600_000_000, 4_000_000),
    )
    back = lax.all_to_all(back, GROUP, 0, 0, tiled=True)

    share = call(drop_place(share_kernel), place, (back,), shape(32, 4, 128), **params(1_000_000, 700_000))
    share = lax.all_to_all(share, LON, 0, 0, tiled=True)
    grad_in = call(
        inverse_kernel,
        place,
        (back, high, low, lat_weight.reshape(rows, 1)),
        shape(group, rows, points),
        picked=(1, 2),
        **params(600_000_000, 4_000_000),
    )
    grad_weight = share.reshape(32, 512)[:, :].reshape(32, 2, 256)[..., : group * WIDE]
    grad_weight = grad_weight.reshape(32, 2, group, WIDE)[..., :rows]
    grad_weight = grad_weight.transpose(3, 1, 0, 2).reshape(rows, 2, channels)
    return (grad_in, grad_weight)


def solution(mesh):
    fine = Mesh(mesh.devices.reshape(SIZES), NAMES)
    return jax.shard_map(
        local,
        mesh=fine,
        in_specs=(P(LON, LAT, None), P(LAT, LON, None, None), P(), P(LON, LAT, None), P(LAT)),
        out_specs=(P(LON, LAT, None), P(LAT, None, None)),
        check_vma=False,
    )
```

```python
import functools
import math

import jax
import jax.numpy as jnp
import ml_dtypes
import numpy as np
from jax import lax
from jax.experimental import pallas as pl
from jax.experimental.pallas import tpu as pltpu
from jax.sharding import Mesh, PartitionSpec as P

NAMES = ("yh", "zh", "zl", "yl", "x", "c")
SIZES = (2, 4, 2, 4, 4, 2)
LAT = ("yh", "zh", "zl")
LON = ("yl", "x", "c")
GROUP = ("yh", "zh", "yl", "x")
BF = jnp.bfloat16
F32 = jnp.float32
WIDE = 48
HALF = WIDE // 2
SAVED = 768
PICK = (((0,), (1,)), ((), ()))
NN = (((1,), (0,)), ((), ()))
NT = (((1,), (1,)), ((), ()))
TN = (((0,), (0,)), ((), ()))


@functools.cache
def tables(points):
    yh, zh, yl, x = (n.reshape(-1) for n in np.meshgrid(*map(np.arange, (2, 4, 4, 4)), indexing="ij"))
    m = 3 * ((yl * 4 + x) * 2 + yh) + zh
    phase = (m[:, None] * np.arange(points)[None]) % points
    angle = 2.0 * math.pi / points * phase
    rows = np.stack([np.cos(angle), -np.sin(angle)]) / math.sqrt(points)
    full = np.where(zh[None, :, None] < 3, rows, 0.0).reshape(256, points).astype(np.float32)
    high = full.astype(ml_dtypes.bfloat16)
    low = (full - high.astype(np.float32)).astype(ml_dtypes.bfloat16)
    return high, low


def channel_slots(channels):
    per = channels // 32
    c, j, b = np.meshgrid(np.arange(2), np.arange(per), np.arange(16), indexing="ij")
    return ((b * 2 + c) * per + j).reshape(2, channels // 2).astype(np.int32)


def dot(a, b, dims):
    return lax.dot_general(a, b, dims, preferred_element_type=F32)


def two(x):
    high = x.astype(BF)
    return high, (x - high.astype(F32)).astype(BF)


def three(x):
    high, rest = x.astype(BF), None
    rest = x - high.astype(F32)
    mid = rest.astype(BF)
    return high, mid, (rest - mid.astype(F32)).astype(BF)


def prepare_kernel(leg_ref, saved_ref, out_ref):
    orders, rows, degrees = leg_ref.shape
    channels = saved_ref.shape[3]
    out_ref[...] = jnp.zeros_like(out_ref)
    for side in range(2):
        n = min(HALF, rows - side * HALF)
        at = slice(side * HALF, side * HALF + n)
        for k in range(orders):
            out_ref[side, k, :n, :degrees] = leg_ref[k, at, :]
            for r in range(2):
                lane = SAVED + r * channels
                out_ref[side, k, :n, lane : lane + channels] = saved_ref[at, k, r, :]


def picks(slots_ref, channels):
    n = slots_ref.shape[1]
    return (lax.broadcasted_iota(jnp.int32, (channels, n), 0) == slots_ref[...]).astype(F32).astype(BF)


def weight_kernel(slots_ref, w_ref, out_ref):
    _, channels, _ = w_ref.shape
    half = channels // 2
    pick = picks(slots_ref, channels)
    for r in range(2):
        out_ref[r * half : (r + 1) * half, :] = sum(dot(pick, term, TN) for term in three(w_ref[r]))


def forward_kernel(g_ref, th_ref, tl_ref, out_ref, field):
    group, rows, points = g_ref.shape
    field[...] = jnp.zeros_like(field)
    for j in range(group):
        field[j * WIDE : j * WIDE + rows, :] = g_ref[j]
    high, low = two(field[...])
    table = th_ref[...]
    acc = dot(table, high, NT) + dot(table, low, NT) + dot(tl_ref[...], high, NT)
    for r in range(2):
        for k in range(2):
            out_ref[:, 2 * r + k, :] = acc[r * 128 : (r + 1) * 128, k * 128 : (k + 1) * 128]


def split_kernel(place_ref, slots_ref, near_ref, far_ref, lh_ref, ll_ref, sv_ref, both):
    degrees = lh_ref.shape[1]
    half = sv_ref.shape[0] // 2
    channels = 2 * half
    rows = degrees // 16
    c = place_ref[0]
    both[:, pl.ds(pl.multiple_of(c * HALF, HALF), HALF), :] = near_ref[...]
    both[:, pl.ds(pl.multiple_of((1 - c) * HALF, HALF), HALF), :] = far_ref[...]
    high, low = two(both[:, :, :degrees].reshape(8 * WIDE, degrees))
    lh_ref[...] = high
    ll_ref[...] = low
    pick = picks(slots_ref, channels)
    for r in range(2):
        lane = SAVED + r * channels
        v = both[:, :, lane : lane + channels].reshape(8 * WIDE, channels)
        mine = sum(dot(pick, term, PICK) for term in three(v))
        for a in range(8):
            piece = mine[:, a * WIDE : a * WIDE + rows]
            for side in range(2):
                at = (2 * a + side) * rows
                sv_ref[r * half : (r + 1) * half, at : at + rows] = piece


def analysis_kernel(x_ref, lh_ref, ll_ref, out_ref, ct, tmp):
    for k in range(4):
        tmp[:, k * 128 : (k + 1) * 128] = x_ref[:, k, :]
    for a in range(8):
        for r in range(2):
            for j in range(5):
                q = (r * 5 + j) * 16
                lane = r * 256 + j * WIDE
                ct[q : q + 16, a * WIDE : (a + 1) * WIDE] = tmp[a * 16 : a * 16 + 16, lane : lane + WIDE]
    ch, cl = two(ct[...])
    n = ch.shape[0]
    both = dot(jnp.concatenate([ch, cl], axis=0), lh_ref[...], NN)
    out_ref[...] = both[:n] + both[n:] + dot(ch, ll_ref[...], NN)


def synthesis_kernel(place_ref, near_ref, far_ref, lh_ref, ll_ref, sv_ref, w_ref, out_ref, back):
    half, degrees = sv_ref.shape[0] // 2, sv_ref.shape[1]
    n, rows = 2 * half, degrees // 16
    back[...] = jnp.zeros_like(back)
    spec = near_ref[...] + far_ref[...]
    g, h = spec[:half], spec[half:]
    u, v = w_ref[:half, :], w_ref[half:, :]
    twice = jnp.where(place_ref[2] == 1, 1.0, 2.0).astype(F32)
    adjoint = jnp.concatenate([(u * g + v * h) * twice, (u * h - v * g) * twice], axis=0)
    p, q = sv_ref[:half, :], sv_ref[half:, :]
    part = (p * g + q * h, p * h - q * g)
    ah, al = two(adjoint)
    both = dot(jnp.concatenate([ah, al], axis=0), lh_ref[...], NT)
    syn = both[:n] + both[n:] + dot(ah, ll_ref[...], NT)
    zl = place_ref[1]
    for a in range(8):
        to = slice(a * 16, a * 16 + 16)
        for r in range(2):
            for j in range(5):
                at = (r * 5 + j) * 16
                lane = r * 256 + j * WIDE
                back[to, lane : lane + WIDE] = syn[at : at + 16, a * WIDE : (a + 1) * WIDE]
                pair = part[r][j * 16 : j * 16 + 16, 2 * a * rows : (2 * a + 2) * rows]
                back[to, 512 + lane : 512 + lane + rows] = jnp.where(zl == 0, pair[:, :rows], pair[:, rows:])
    for k in range(8):
        out_ref[:, k, :] = back[:, k * 128 : (k + 1) * 128]


def share_kernel(x_ref, out_ref):
    total = jnp.sum(x_ref[...], axis=0)[4:8]
    out_ref[...] = jnp.broadcast_to(total[None], out_ref.shape)


def inverse_kernel(x_ref, th_ref, tl_ref, lw_ref, out_ref):
    group, rows, points = out_ref.shape
    block = jnp.concatenate(
        [jnp.concatenate([x_ref[:, 2 * r, :], x_ref[:, 2 * r + 1, :]], axis=1) for r in range(2)], axis=0
    )
    high, low = two(block)
    table = th_ref[...]
    acc = dot(high, table, TN) + dot(low, table, TN) + dot(high, tl_ref[...], TN)
    for j in range(group):
        out_ref[j] = acc[j * WIDE : j * WIDE + rows] * lw_ref[...]


def call(kernel, args, out_shapes, flops, scratch=(), scalars=0, hbm_out=False):
    vmem = pl.BlockSpec(memory_space=pltpu.VMEM)
    smem = pl.BlockSpec(memory_space=pltpu.SMEM)
    moved = sum(a.size * a.dtype.itemsize for a in (*args, *jax.tree.leaves(out_shapes)))
    extra = {} if hbm_out else dict(out_specs=jax.tree.map(lambda s: vmem, out_shapes))
    return pl.pallas_call(
        kernel,
        out_shape=out_shapes,
        in_specs=[smem if i < scalars else vmem for i in range(len(args))],
        scratch_shapes=list(scratch),
        compiler_params=pltpu.CompilerParams(vmem_limit_bytes=24 * 2**20),
        cost_estimate=pl.CostEstimate(flops=flops, bytes_accessed=moved, transcendentals=0),
        **extra,
    )(*args)


def shape(*dims, dtype=F32):
    return jax.ShapeDtypeStruct(dims, dtype)


def local(grad_out, saved_spectra, spec_weight, legendre, lat_weight):
    group, rows, points = grad_out.shape
    degrees, _, channels = spec_weight.shape
    orders = legendre.shape[0]
    half = channels // 2
    yh, zh, zl, yl, x, c = (lax.axis_index(n) for n in NAMES)
    first = yh + zh + yl + x == 0
    place = jnp.stack([c, zl, first.astype(jnp.int32)]).astype(jnp.int32)
    slot_table = jnp.asarray(channel_slots(channels))
    slots = jnp.where(c == 0, slot_table[0:1], slot_table[1:2])
    high, low = (jnp.asarray(t) for t in tables(points))

    rows_out = call(
        prepare_kernel,
        (legendre, saved_spectra),
        shape(2, orders + 1, HALF, SAVED + 3 * 128),
        1000,
    )
    rows_out = lax.all_to_all(rows_out, ("c",), 0, 0, tiled=True)
    near = lax.all_to_all(rows_out.reshape(8, HALF, -1), ("yh", "zh"), 0, 0, tiled=True)

    coeffs = call(
        forward_kernel,
        (grad_out, high, low),
        shape(128, 4, 128),
        600_000_000,
        scratch=[pltpu.VMEM((256, points), F32)],
    )
    weight = call(weight_kernel, (slots, spec_weight.transpose(1, 2, 0)), shape(2 * half, degrees), 100_000_000)
    coeffs, weight, near = lax.optimization_barrier((coeffs, weight, near))
    far = lax.ppermute(near, ("c",), [(0, 1), (1, 0)])
    coeffs = lax.all_to_all(coeffs, GROUP, 0, 0, tiled=True)
    leg_high, leg_low, sv = call(
        split_kernel,
        (place, slots, near, far),
        (
            shape(8 * WIDE, degrees, dtype=BF),
            shape(8 * WIDE, degrees, dtype=BF),
            shape(2 * half, degrees),
        ),
        100_000_000,
        scratch=[pltpu.VMEM((8, WIDE, SAVED + 3 * 128), F32)],
        scalars=1,
    )
    spectra = call(
        analysis_kernel,
        (coeffs, leg_high, leg_low),
        shape(2 * half, degrees),
        300_000_000,
        scratch=[pltpu.VMEM((2 * half, 8 * WIDE), F32), pltpu.VMEM((128, 512), F32)],
    )
    other = lax.ppermute(spectra, ("zl",), [(0, 1), (1, 0)])
    back = call(
        synthesis_kernel,
        (place, spectra, other, leg_high, leg_low, sv, weight),
        shape(128, 8, 128),
        300_000_000,
        scratch=[pltpu.VMEM((128, 1024), F32)],
        scalars=1,
    )
    back = lax.all_to_all(back, GROUP, 0, 0, tiled=True)

    share = call(share_kernel, (back,), shape(32, 4, 128), 1_000_000)
    share = lax.all_to_all(share, LON, 0, 0, tiled=True)
    grad_in = call(
        inverse_kernel,
        (back, high, low, lat_weight.reshape(rows, 1)),
        shape(group, rows, points),
        600_000_000,
        hbm_out=True,
    )
    grad_weight = share.reshape(32, 2, 256)[..., : group * WIDE].reshape(32, 2, group, WIDE)[..., :rows]
    grad_weight = grad_weight.transpose(3, 1, 0, 2).reshape(rows, 2, channels)
    return (grad_in, grad_weight)


def solution(mesh):
    fine = Mesh(mesh.devices.reshape(SIZES), NAMES)
    return jax.shard_map(
        local,
        mesh=fine,
        in_specs=(P(LON, LAT, None), P(LAT, LON, None, None), P(), P(LON, LAT, None), P(LAT)),
        out_specs=(P(LON, LAT, None), P(LAT, None, None)),
        check_vma=False,
    )
```

```python
import functools
import math

import jax
import jax.numpy as jnp
import ml_dtypes
import numpy as np
from jax import lax
from jax.experimental import pallas as pl
from jax.experimental.pallas import tpu as pltpu
from jax.sharding import Mesh, PartitionSpec as P

NAMES = ("yh", "z", "yl", "x", "c")
SIZES = (2, 8, 4, 4, 2)
LAT = ("yh", "z")
LON = ("yl", "x", "c")
GROUP = ("z", "yl", "x")
BF = jnp.bfloat16
F32 = jnp.float32
WIDE = 48
HALF = WIDE // 2
SAVED = 768
PICK = (((0,), (1,)), ((), ()))
NN = (((1,), (0,)), ((), ()))
NT = (((1,), (1,)), ((), ()))
TN = (((0,), (0,)), ((), ()))


@functools.cache
def tables(points):
    z, yl, x = (n.reshape(-1) for n in np.meshgrid(*map(np.arange, (8, 4, 4)), indexing="ij"))
    m = 3 * ((yl * 4 + x) * 2 + z // 4) + z % 4
    phase = (m[:, None] * np.arange(points)[None]) % points
    angle = 2.0 * math.pi / points * phase
    rows = np.stack([np.cos(angle), -np.sin(angle)]) / math.sqrt(points)
    full = np.where(z[None, :, None] % 4 < 3, rows, 0.0).reshape(256, points).astype(np.float32)
    high = full.astype(ml_dtypes.bfloat16)
    low = (full - high.astype(np.float32)).astype(ml_dtypes.bfloat16)
    return high, low


def channel_slots(channels):
    per = channels // 32
    c, j, b = np.meshgrid(np.arange(2), np.arange(per), np.arange(16), indexing="ij")
    return ((b * 2 + c) * per + j).reshape(2, channels // 2).astype(np.int32)


def dot(a, b, dims):
    return lax.dot_general(a, b, dims, preferred_element_type=F32)


def two(x):
    high = x.astype(BF)
    return high, (x - high.astype(F32)).astype(BF)


def three(x):
    high, rest = x.astype(BF), None
    rest = x - high.astype(F32)
    mid = rest.astype(BF)
    return high, mid, (rest - mid.astype(F32)).astype(BF)


def prepare_kernel(leg_ref, saved_ref, out_ref):
    orders, rows, degrees = leg_ref.shape
    channels = saved_ref.shape[3]
    out_ref[...] = jnp.zeros_like(out_ref)
    for side in range(2):
        n = min(HALF, rows - side * HALF)
        at = slice(side * HALF, side * HALF + n)
        for k in range(orders):
            out_ref[side, k, :n, :degrees] = leg_ref[k, at, :]
            for r in range(2):
                lane = SAVED + r * channels
                out_ref[side, k, :n, lane : lane + channels] = saved_ref[at, k, r, :]


def picks(slots_ref, channels):
    n = slots_ref.shape[1]
    return (lax.broadcasted_iota(jnp.int32, (channels, n), 0) == slots_ref[...]).astype(F32).astype(BF)


def weight_kernel(slots_ref, w_ref, out_ref):
    _, channels, _ = w_ref.shape
    half = channels // 2
    pick = picks(slots_ref, channels)
    for r in range(2):
        out_ref[r * half : (r + 1) * half, :] = sum(dot(pick, term, TN) for term in three(w_ref[r]))


def forward_kernel(g_ref, th_ref, tl_ref, out_ref, field):
    group, rows, points = g_ref.shape
    field[...] = jnp.zeros_like(field)
    for j in range(group):
        field[j * WIDE : j * WIDE + rows, :] = g_ref[j]
    high, low = two(field[...])
    table = th_ref[...]
    acc = dot(table, high, NT) + dot(table, low, NT) + dot(tl_ref[...], high, NT)
    for r in range(2):
        for k in range(2):
            out_ref[:, 2 * r + k, :] = acc[r * 128 : (r + 1) * 128, k * 128 : (k + 1) * 128]


def split_kernel(place_ref, slots_ref, near_ref, far_ref, lh_ref, ll_ref, sv_ref, both):
    degrees = lh_ref.shape[1]
    half = sv_ref.shape[0] // 2
    channels = 2 * half
    rows = degrees // 16
    c = place_ref[0]
    both[:, pl.ds(pl.multiple_of(c * HALF, HALF), HALF), :] = near_ref[...]
    both[:, pl.ds(pl.multiple_of((1 - c) * HALF, HALF), HALF), :] = far_ref[...]
    high, low = two(both[:, :, :degrees].reshape(8 * WIDE, degrees))
    lh_ref[...] = high
    ll_ref[...] = low
    pick = picks(slots_ref, channels)
    for r in range(2):
        lane = SAVED + r * channels
        v = both[:, :, lane : lane + channels].reshape(8 * WIDE, channels)
        mine = sum(dot(pick, term, PICK) for term in three(v))
        for a in range(8):
            sv_ref[r * half : (r + 1) * half, a * rows : (a + 1) * rows] = mine[:, a * WIDE : a * WIDE + rows]


def analysis_kernel(x_ref, lh_ref, ll_ref, out_ref, ct, tmp):
    for k in range(4):
        tmp[:, k * 128 : (k + 1) * 128] = x_ref[:, k, :]
    for a in range(8):
        for r in range(2):
            for j in range(5):
                q = (r * 5 + j) * 16
                lane = r * 256 + j * WIDE
                ct[q : q + 16, a * WIDE : (a + 1) * WIDE] = tmp[a * 16 : a * 16 + 16, lane : lane + WIDE]
    ch, cl = two(ct[...])
    n = ch.shape[0]
    both = dot(jnp.concatenate([ch, cl], axis=0), lh_ref[...], NN)
    out_ref[...] = both[:n] + both[n:] + dot(ch, ll_ref[...], NN)


def synthesis_kernel(place_ref, near_ref, far_ref, lh_ref, ll_ref, sv_ref, w_ref, out_ref, back):
    half, degrees = w_ref.shape[0] // 2, w_ref.shape[1]
    n, rows = 2 * half, degrees // 16
    back[...] = jnp.zeros_like(back)
    spec = near_ref[...] + far_ref[...]
    g, h = spec[:half], spec[half:]
    u, v = w_ref[:half, :], w_ref[half:, :]
    twice = jnp.where(place_ref[2] == 1, 1.0, 2.0).astype(F32)
    adjoint = jnp.concatenate([(u * g + v * h) * twice, (u * h - v * g) * twice], axis=0)
    p, q = sv_ref[:half, :], sv_ref[half:, :]
    own = jnp.where(place_ref[1] == 0, spec[:, : degrees // 2], spec[:, degrees // 2 :])
    g, h = own[:half], own[half:]
    part = (p * g + q * h, p * h - q * g)
    ah, al = two(adjoint)
    both = dot(jnp.concatenate([ah, al], axis=0), lh_ref[...], NT)
    syn = both[:n] + both[n:] + dot(ah, ll_ref[...], NT)
    for a in range(8):
        to = slice(a * 16, a * 16 + 16)
        for r in range(2):
            for j in range(5):
                at = (r * 5 + j) * 16
                lane = r * 256 + j * WIDE
                back[to, lane : lane + WIDE] = syn[at : at + 16, a * WIDE : (a + 1) * WIDE]
                piece = part[r][j * 16 : j * 16 + 16, a * rows : (a + 1) * rows]
                back[to, 512 + lane : 512 + lane + rows] = piece
    for k in range(8):
        out_ref[:, k, :] = back[:, k * 128 : (k + 1) * 128]


def share_kernel(x_ref, out_ref):
    total = jnp.sum(x_ref[...], axis=0)[4:8]
    out_ref[...] = jnp.broadcast_to(total[None], out_ref.shape)


def inverse_kernel(x_ref, th_ref, tl_ref, lw_ref, out_ref):
    group, rows, points = out_ref.shape
    block = jnp.concatenate(
        [jnp.concatenate([x_ref[:, 2 * r, :], x_ref[:, 2 * r + 1, :]], axis=1) for r in range(2)], axis=0
    )
    high, low = two(block)
    table = th_ref[...]
    acc = dot(high, table, TN) + dot(low, table, TN) + dot(high, tl_ref[...], TN)
    for j in range(group):
        out_ref[j] = acc[j * WIDE : j * WIDE + rows] * lw_ref[...]


def call(kernel, args, out_shapes, flops, scratch=(), scalars=0, hbm_out=False):
    vmem = pl.BlockSpec(memory_space=pltpu.VMEM)
    smem = pl.BlockSpec(memory_space=pltpu.SMEM)
    moved = sum(a.size * a.dtype.itemsize for a in (*args, *jax.tree.leaves(out_shapes)))
    extra = {} if hbm_out else dict(out_specs=jax.tree.map(lambda s: vmem, out_shapes))
    return pl.pallas_call(
        kernel,
        out_shape=out_shapes,
        in_specs=[smem if i < scalars else vmem for i in range(len(args))],
        scratch_shapes=list(scratch),
        compiler_params=pltpu.CompilerParams(vmem_limit_bytes=24 * 2**20),
        cost_estimate=pl.CostEstimate(flops=flops, bytes_accessed=moved, transcendentals=0),
        **extra,
    )(*args)


def shape(*dims, dtype=F32):
    return jax.ShapeDtypeStruct(dims, dtype)


def local(grad_out, saved_spectra, spec_weight, legendre, lat_weight):
    group, rows, points = grad_out.shape
    degrees, _, channels = spec_weight.shape
    orders = legendre.shape[0]
    half = channels // 2
    yh, z, yl, x, c = (lax.axis_index(n) for n in NAMES)
    first = z + yl + x == 0
    place = jnp.stack([c, yh, first.astype(jnp.int32)]).astype(jnp.int32)
    slot_table = jnp.asarray(channel_slots(channels))
    slots = jnp.where(c == 0, slot_table[0:1], slot_table[1:2])
    high, low = (jnp.asarray(t) for t in tables(points))

    rows_out = call(
        prepare_kernel,
        (legendre, saved_spectra),
        shape(2, orders + 1, HALF, SAVED + 3 * 128),
        1000,
    )
    rows_out = lax.all_to_all(rows_out, ("c",), 0, 0, tiled=True)
    near = lax.all_to_all(rows_out.reshape(8, HALF, -1), ("z",), 0, 0, tiled=True)

    coeffs = call(
        forward_kernel,
        (grad_out, high, low),
        shape(128, 4, 128),
        600_000_000,
        scratch=[pltpu.VMEM((256, points), F32)],
    )
    weight = call(weight_kernel, (slots, spec_weight.transpose(1, 2, 0)), shape(2 * half, degrees), 100_000_000)
    coeffs, weight, near = lax.optimization_barrier((coeffs, weight, near))
    far = lax.ppermute(near, ("c",), [(0, 1), (1, 0)])
    coeffs = lax.all_to_all(coeffs, GROUP, 0, 0, tiled=True)
    leg_high, leg_low, sv = call(
        split_kernel,
        (place, slots, near, far),
        (
            shape(8 * WIDE, degrees, dtype=BF),
            shape(8 * WIDE, degrees, dtype=BF),
            shape(2 * half, degrees // 2),
        ),
        100_000_000,
        scratch=[pltpu.VMEM((8, WIDE, SAVED + 3 * 128), F32)],
        scalars=1,
    )
    spectra = call(
        analysis_kernel,
        (coeffs, leg_high, leg_low),
        shape(2 * half, degrees),
        300_000_000,
        scratch=[pltpu.VMEM((2 * half, 8 * WIDE), F32), pltpu.VMEM((128, 512), F32)],
    )
    other = lax.ppermute(spectra, ("yh",), [(0, 1), (1, 0)])
    back = call(
        synthesis_kernel,
        (place, spectra, other, leg_high, leg_low, sv, weight),
        shape(128, 8, 128),
        300_000_000,
        scratch=[pltpu.VMEM((128, 1024), F32)],
        scalars=1,
    )
    back = lax.all_to_all(back, GROUP, 0, 0, tiled=True)

    share = call(share_kernel, (back,), shape(32, 4, 128), 1_000_000)
    share = lax.all_to_all(share, LON, 0, 0, tiled=True)
    grad_in = call(
        inverse_kernel,
        (back, high, low, lat_weight.reshape(rows, 1)),
        shape(group, rows, points),
        600_000_000,
        hbm_out=True,
    )
    grad_weight = share.reshape(32, 2, 256)[..., : group * WIDE].reshape(32, 2, group, WIDE)[..., :rows]
    grad_weight = grad_weight.transpose(3, 1, 0, 2).reshape(rows, 2, channels)
    return (grad_in, grad_weight)


def solution(mesh):
    fine = Mesh(mesh.devices.reshape(SIZES), NAMES)
    return jax.shard_map(
        local,
        mesh=fine,
        in_specs=(P(LON, LAT, None), P(LAT, LON, None, None), P(), P(LON, LAT, None), P(LAT)),
        out_specs=(P(LON, LAT, None), P(LAT, None, None)),
        check_vma=False,
    )
```

```python
import functools
import math

import jax
import jax.numpy as jnp
import ml_dtypes
import numpy as np
from jax import lax
from jax.experimental import pallas as pl
from jax.experimental.pallas import tpu as pltpu
from jax.sharding import Mesh, PartitionSpec as P

NAMES = ("yh", "z", "yl", "x", "c")
SIZES = (2, 8, 4, 4, 2)
LAT = ("yh", "z")
LON = ("yl", "x", "c")
GROUP = ("z", "yl", "x")
BF = jnp.bfloat16
F32 = jnp.float32
WIDE = 48
HALF = WIDE // 2
TOP = HALF - 1
PICK = (((0,), (1,)), ((), ()))
NN = (((1,), (0,)), ((), ()))
NT = (((1,), (1,)), ((), ()))
TN = (((0,), (0,)), ((), ()))


@functools.cache
def tables(points):
    z, yl, x = (n.reshape(-1) for n in np.meshgrid(*map(np.arange, (8, 4, 4)), indexing="ij"))
    m = 3 * ((yl * 4 + x) * 2 + z // 4) + z % 4
    phase = (m[:, None] * np.arange(points)[None]) % points
    angle = 2.0 * math.pi / points * phase
    rows = np.stack([np.cos(angle), -np.sin(angle)]) / math.sqrt(points)
    full = np.where(z[None, :, None] % 4 < 3, rows, 0.0).reshape(256, points).astype(np.float32)
    high = full.astype(ml_dtypes.bfloat16)
    low = (full - high.astype(np.float32)).astype(ml_dtypes.bfloat16)
    return high, low


def channel_slots(channels):
    per = channels // 32
    c, j, b = np.meshgrid(np.arange(2), np.arange(per), np.arange(16), indexing="ij")
    return ((b * 2 + c) * per + j).reshape(2, channels // 2).astype(np.int32)


def dot(a, b, dims):
    return lax.dot_general(a, b, dims, preferred_element_type=F32)


def two(x):
    high = x.astype(BF)
    return high, (x - high.astype(F32)).astype(BF)


def three(x):
    high, rest = x.astype(BF), None
    rest = x - high.astype(F32)
    mid = rest.astype(BF)
    return high, mid, (rest - mid.astype(F32)).astype(BF)


def prepare_kernel(leg_ref, saved_ref, out_ref):
    orders, rows, degrees = leg_ref.shape
    channels = saved_ref.shape[3]
    lanes = out_ref.shape[3]
    fit = lanes - degrees - channels
    rest = channels - fit
    out_ref[...] = jnp.zeros_like(out_ref)
    for side, (low, n) in enumerate(((0, TOP), (TOP, rows - TOP))):
        at = slice(low, low + n)
        for k in range(orders):
            out_ref[side, k, :n, :degrees] = leg_ref[k, at, :]
            out_ref[side, k, :n, degrees : degrees + channels] = saved_ref[at, k, 0, :]
            out_ref[side, k, :n, degrees + channels :] = saved_ref[at, k, 1, :fit]
            for i in range(n):
                tail = saved_ref[low + i : low + i + 1, k, 1, fit:]
                out_ref[side, k, TOP:HALF, i * rest : (i + 1) * rest] = tail


def picks(slots_ref, channels):
    n = slots_ref.shape[1]
    return (lax.broadcasted_iota(jnp.int32, (channels, n), 0) == slots_ref[...]).astype(F32).astype(BF)


def weight_kernel(slots_ref, w_ref, out_ref):
    _, channels, _ = w_ref.shape
    half = channels // 2
    pick = picks(slots_ref, channels)
    for r in range(2):
        out_ref[r * half : (r + 1) * half, :] = sum(dot(pick, term, TN) for term in three(w_ref[r]))


def forward_kernel(g_ref, th_ref, tl_ref, out_ref, field):
    group, rows, points = g_ref.shape
    field[...] = jnp.zeros_like(field)
    for j in range(group):
        field[j * WIDE : j * WIDE + TOP, :] = g_ref[j, :TOP, :]
        field[j * WIDE + HALF : j * WIDE + HALF + rows - TOP, :] = g_ref[j, TOP:, :]
    high, low = two(field[...])
    table = th_ref[...]
    acc = dot(table, high, NT) + dot(table, low, NT) + dot(tl_ref[...], high, NT)
    for r in range(2):
        for k in range(2):
            out_ref[:, 2 * r + k, :] = acc[r * 128 : (r + 1) * 128, k * 128 : (k + 1) * 128]


def split_kernel(place_ref, slots_ref, near_ref, far_ref, lh_ref, ll_ref, sv_ref, both, second):
    degrees = lh_ref.shape[1]
    half = sv_ref.shape[0] // 2
    channels = 2 * half
    rows = degrees // 16
    fit = both.shape[2] - degrees - channels
    rest = channels - fit
    c = place_ref[0]
    both[:, pl.ds(pl.multiple_of(c * HALF, HALF), HALF), :] = near_ref[...]
    both[:, pl.ds(pl.multiple_of((1 - c) * HALF, HALF), HALF), :] = far_ref[...]
    high, low = two(both[:, :, :degrees].reshape(8 * WIDE, degrees))
    lh_ref[...] = high
    ll_ref[...] = low
    second[...] = jnp.zeros_like(second)
    second[:, :, :fit] = both[:, :, degrees + channels :]
    for side, n in enumerate((TOP, rows - TOP)):
        for i in range(n):
            second[:, side * HALF + i, fit:] = both[:, side * HALF + TOP, i * rest : (i + 1) * rest]
    pick = picks(slots_ref, channels)
    for r, v in enumerate((both[:, :, degrees : degrees + channels], second[...])):
        mine = sum(dot(pick, term, PICK) for term in three(v.reshape(8 * WIDE, channels)))
        to = slice(r * half, (r + 1) * half)
        for a in range(8):
            at, src = a * rows, a * WIDE
            sv_ref[to, at : at + TOP] = mine[:, src : src + TOP]
            sv_ref[to, at + TOP : at + rows] = mine[:, src + HALF : src + HALF + rows - TOP]


def analysis_kernel(x_ref, lh_ref, ll_ref, out_ref, ct, tmp):
    for k in range(4):
        tmp[:, k * 128 : (k + 1) * 128] = x_ref[:, k, :]
    for a in range(8):
        for r in range(2):
            for j in range(5):
                q = (r * 5 + j) * 16
                lane = r * 256 + j * WIDE
                ct[q : q + 16, a * WIDE : (a + 1) * WIDE] = tmp[a * 16 : a * 16 + 16, lane : lane + WIDE]
    ch, cl = two(ct[...])
    n = ch.shape[0]
    both = dot(jnp.concatenate([ch, cl], axis=0), lh_ref[...], NN)
    out_ref[...] = both[:n] + both[n:] + dot(ch, ll_ref[...], NN)


def synthesis_kernel(place_ref, near_ref, far_ref, lh_ref, ll_ref, sv_ref, w_ref, out_ref, back):
    half, degrees = w_ref.shape[0] // 2, w_ref.shape[1]
    n, rows = 2 * half, degrees // 16
    back[...] = jnp.zeros_like(back)
    spec = near_ref[...] + far_ref[...]
    g, h = spec[:half], spec[half:]
    u, v = w_ref[:half, :], w_ref[half:, :]
    twice = jnp.where(place_ref[2] == 1, 1.0, 2.0).astype(F32)
    adjoint = jnp.concatenate([(u * g + v * h) * twice, (u * h - v * g) * twice], axis=0)
    p, q = sv_ref[:half, :], sv_ref[half:, :]
    own = jnp.where(place_ref[1] == 0, spec[:, : degrees // 2], spec[:, degrees // 2 :])
    g, h = own[:half], own[half:]
    part = (p * g + q * h, p * h - q * g)
    ah, al = two(adjoint)
    both = dot(jnp.concatenate([ah, al], axis=0), lh_ref[...], NT)
    syn = both[:n] + both[n:] + dot(ah, ll_ref[...], NT)
    for a in range(8):
        to = slice(a * 16, a * 16 + 16)
        for r in range(2):
            for j in range(5):
                at = (r * 5 + j) * 16
                lane = r * 256 + j * WIDE
                back[to, lane : lane + WIDE] = syn[at : at + 16, a * WIDE : (a + 1) * WIDE]
                piece = part[r][j * 16 : j * 16 + 16, a * rows : (a + 1) * rows]
                back[to, 512 + lane : 512 + lane + rows] = piece
    for k in range(8):
        out_ref[:, k, :] = back[:, k * 128 : (k + 1) * 128]


def share_kernel(x_ref, out_ref):
    total = jnp.sum(x_ref[...], axis=0)[4:8]
    out_ref[...] = jnp.broadcast_to(total[None], out_ref.shape)


def inverse_kernel(x_ref, th_ref, tl_ref, lw_ref, out_ref):
    group, rows, points = out_ref.shape
    block = jnp.concatenate(
        [jnp.concatenate([x_ref[:, 2 * r, :], x_ref[:, 2 * r + 1, :]], axis=1) for r in range(2)], axis=0
    )
    high, low = two(block)
    table = th_ref[...]
    acc = dot(high, table, TN) + dot(low, table, TN) + dot(high, tl_ref[...], TN)
    for j in range(group):
        at = j * WIDE
        out_ref[j, :TOP, :] = acc[at : at + TOP] * lw_ref[:TOP, :]
        out_ref[j, TOP:, :] = acc[at + HALF : at + HALF + rows - TOP] * lw_ref[TOP:, :]


def call(kernel, args, out_shapes, flops, scratch=(), scalars=0, hbm_out=False):
    vmem = pl.BlockSpec(memory_space=pltpu.VMEM)
    smem = pl.BlockSpec(memory_space=pltpu.SMEM)
    moved = sum(a.size * a.dtype.itemsize for a in (*args, *jax.tree.leaves(out_shapes)))
    extra = {} if hbm_out else dict(out_specs=jax.tree.map(lambda s: vmem, out_shapes))
    return pl.pallas_call(
        kernel,
        out_shape=out_shapes,
        in_specs=[smem if i < scalars else vmem for i in range(len(args))],
        scratch_shapes=list(scratch),
        compiler_params=pltpu.CompilerParams(vmem_limit_bytes=24 * 2**20),
        cost_estimate=pl.CostEstimate(flops=flops, bytes_accessed=moved, transcendentals=0),
        **extra,
    )(*args)


def shape(*dims, dtype=F32):
    return jax.ShapeDtypeStruct(dims, dtype)


def local(grad_out, saved_spectra, spec_weight, legendre, lat_weight):
    group, rows, points = grad_out.shape
    degrees, _, channels = spec_weight.shape
    orders = legendre.shape[0]
    half = channels // 2
    yh, z, yl, x, c = (lax.axis_index(n) for n in NAMES)
    first = z + yl + x == 0
    place = jnp.stack([c, yh, first.astype(jnp.int32)]).astype(jnp.int32)
    slot_table = jnp.asarray(channel_slots(channels))
    slots = jnp.where(c == 0, slot_table[0:1], slot_table[1:2])
    high, low = (jnp.asarray(t) for t in tables(points))

    rows_out = call(
        prepare_kernel,
        (legendre, saved_spectra),
        shape(2, orders + 1, HALF, 8 * 128),
        1000,
    )
    rows_out = lax.all_to_all(rows_out, ("c",), 0, 0, tiled=True)
    near = lax.all_to_all(rows_out.reshape(8, HALF, -1), ("z",), 0, 0, tiled=True)

    coeffs = call(
        forward_kernel,
        (grad_out, high, low),
        shape(128, 4, 128),
        600_000_000,
        scratch=[pltpu.VMEM((256, points), F32)],
    )
    weight = call(weight_kernel, (slots, spec_weight.transpose(1, 2, 0)), shape(2 * half, degrees), 100_000_000)
    coeffs, weight, near = lax.optimization_barrier((coeffs, weight, near))
    far = lax.ppermute(near, ("c",), [(0, 1), (1, 0)])
    coeffs = lax.all_to_all(coeffs, GROUP, 0, 0, tiled=True)
    leg_high, leg_low, sv = call(
        split_kernel,
        (place, slots, near, far),
        (
            shape(8 * WIDE, degrees, dtype=BF),
            shape(8 * WIDE, degrees, dtype=BF),
            shape(2 * half, degrees // 2),
        ),
        100_000_000,
        scratch=[pltpu.VMEM((8, WIDE, 8 * 128), F32), pltpu.VMEM((8, WIDE, channels), F32)],
        scalars=1,
    )
    spectra = call(
        analysis_kernel,
        (coeffs, leg_high, leg_low),
        shape(2 * half, degrees),
        300_000_000,
        scratch=[pltpu.VMEM((2 * half, 8 * WIDE), F32), pltpu.VMEM((128, 512), F32)],
    )
    other = lax.ppermute(spectra, ("yh",), [(0, 1), (1, 0)])
    back = call(
        synthesis_kernel,
        (place, spectra, other, leg_high, leg_low, sv, weight),
        shape(128, 8, 128),
        300_000_000,
        scratch=[pltpu.VMEM((128, 1024), F32)],
        scalars=1,
    )
    back = lax.all_to_all(back, GROUP, 0, 0, tiled=True)

    share = call(share_kernel, (back,), shape(32, 4, 128), 1_000_000)
    share = lax.all_to_all(share, LON, 0, 0, tiled=True)
    grad_in = call(
        inverse_kernel,
        (back, high, low, lat_weight.reshape(rows, 1)),
        shape(group, rows, points),
        600_000_000,
        hbm_out=True,
    )
    grad_weight = share.reshape(32, 2, 256)[..., : group * WIDE].reshape(32, 2, group, WIDE)[..., :rows]
    grad_weight = grad_weight.transpose(3, 1, 0, 2).reshape(rows, 2, channels)
    return (grad_in, grad_weight)


def solution(mesh):
    fine = Mesh(mesh.devices.reshape(SIZES), NAMES)
    return jax.shard_map(
        local,
        mesh=fine,
        in_specs=(P(LON, LAT, None), P(LAT, LON, None, None), P(), P(LON, LAT, None), P(LAT)),
        out_specs=(P(LON, LAT, None), P(LAT, None, None)),
        check_vma=False,
    )
```

```python
import functools
import math

import jax
import jax.numpy as jnp
import ml_dtypes
import numpy as np
from jax import lax
from jax.experimental import pallas as pl
from jax.experimental.pallas import tpu as pltpu
from jax.sharding import Mesh, PartitionSpec as P

NAMES = ("yh", "z", "yl", "x", "c")
SIZES = (2, 8, 4, 4, 2)
LAT = ("yh", "z")
LON = ("yl", "x", "c")
GROUP = ("z", "yl", "x")
BF = jnp.bfloat16
F32 = jnp.float32
WIDE = 48
HALF = WIDE // 2
TOP = HALF - 1
PICK = (((0,), (1,)), ((), ()))
NN = (((1,), (0,)), ((), ()))
NT = (((1,), (1,)), ((), ()))
TN = (((0,), (0,)), ((), ()))


@functools.cache
def tables(points):
    z, yl, x = (n.reshape(-1) for n in np.meshgrid(*map(np.arange, (8, 4, 4)), indexing="ij"))
    m = 3 * ((yl * 4 + x) * 2 + z // 4) + z % 4
    phase = (m[:, None] * np.arange(points)[None]) % points
    angle = 2.0 * math.pi / points * phase
    rows = np.stack([np.cos(angle), -np.sin(angle)]) / math.sqrt(points)
    full = np.where(z[None, :, None] % 4 < 3, rows, 0.0).reshape(256, points).astype(np.float32)
    high = full.astype(ml_dtypes.bfloat16)
    low = (full - high.astype(np.float32)).astype(ml_dtypes.bfloat16)
    return high, low


def channel_slots(channels):
    per = channels // 32
    c, j, b = np.meshgrid(np.arange(2), np.arange(per), np.arange(16), indexing="ij")
    return ((b * 2 + c) * per + j).reshape(2, channels // 2).astype(np.int32)


def dot(a, b, dims):
    return lax.dot_general(a, b, dims, preferred_element_type=F32)


def two(x):
    high = x.astype(BF)
    return high, (x - high.astype(F32)).astype(BF)


def three(x):
    high, rest = x.astype(BF), None
    rest = x - high.astype(F32)
    mid = rest.astype(BF)
    return high, mid, (rest - mid.astype(F32)).astype(BF)


def prepare_kernel(leg_ref, saved_ref, out_ref):
    orders, rows, degrees = leg_ref.shape
    channels = saved_ref.shape[3]
    lanes = out_ref.shape[3]
    fit = lanes - degrees - channels
    rest = channels - fit
    out_ref[...] = jnp.zeros_like(out_ref)
    for side, (low, n) in enumerate(((0, TOP), (TOP, rows - TOP))):
        at = slice(low, low + n)
        for k in range(orders):
            out_ref[side, k, :n, :degrees] = leg_ref[k, at, :]
            out_ref[side, k, :n, degrees : degrees + channels] = saved_ref[at, k, 0, :]
            out_ref[side, k, :n, degrees + channels :] = saved_ref[at, k, 1, :fit]
            for i in range(n):
                tail = saved_ref[low + i : low + i + 1, k, 1, fit:]
                out_ref[side, k, TOP:HALF, i * rest : (i + 1) * rest] = tail


def picks(slots_ref, channels):
    n = slots_ref.shape[1]
    return (lax.broadcasted_iota(jnp.int32, (channels, n), 0) == slots_ref[...]).astype(F32).astype(BF)


def weight_kernel(slots_ref, w_ref, out_ref):
    _, channels, _ = w_ref.shape
    half = channels // 2
    pick = picks(slots_ref, channels)
    for r in range(2):
        out_ref[r * half : (r + 1) * half, :] = sum(dot(pick, term, TN) for term in three(w_ref[r]))


def forward_kernel(g_ref, th_ref, tl_ref, out_ref, field):
    group, rows, points = g_ref.shape
    field[...] = jnp.zeros_like(field)
    for j in range(group):
        field[j * WIDE : j * WIDE + TOP, :] = g_ref[j, :TOP, :]
        field[j * WIDE + HALF : j * WIDE + HALF + rows - TOP, :] = g_ref[j, TOP:, :]
    high, low = two(field[...])
    table = th_ref[...]
    acc = dot(table, high, NT) + dot(table, low, NT) + dot(tl_ref[...], high, NT)
    for r in range(2):
        for k in range(2):
            out_ref[:, 2 * r + k, :] = acc[r * 128 : (r + 1) * 128, k * 128 : (k + 1) * 128]


def split_kernel(place_ref, slots_ref, near_ref, far_ref, lh_ref, ll_ref, sv_ref, both, second):
    degrees = lh_ref.shape[1]
    half = sv_ref.shape[0] // 2
    channels = 2 * half
    rows = degrees // 16
    fit = both.shape[2] - degrees - channels
    rest = channels - fit
    c = place_ref[0]
    both[:, pl.ds(pl.multiple_of(c * HALF, HALF), HALF), :] = near_ref[...]
    both[:, pl.ds(pl.multiple_of((1 - c) * HALF, HALF), HALF), :] = far_ref[...]
    high, low = two(both[:, :, :degrees].reshape(8 * WIDE, degrees))
    lh_ref[...] = high
    ll_ref[...] = low
    second[...] = jnp.zeros_like(second)
    second[:, :, :fit] = both[:, :, degrees + channels :]
    for side, n in enumerate((TOP, rows - TOP)):
        for i in range(n):
            second[:, side * HALF + i, fit:] = both[:, side * HALF + TOP, i * rest : (i + 1) * rest]
    pick = picks(slots_ref, channels)
    for r, v in enumerate((both[:, :, degrees : degrees + channels], second[...])):
        mine = sum(dot(pick, term, PICK) for term in three(v.reshape(8 * WIDE, channels)))
        to = slice(r * half, (r + 1) * half)
        for a in range(8):
            at, src = a * rows, a * WIDE
            sv_ref[to, at : at + TOP] = mine[:, src : src + TOP]
            sv_ref[to, at + TOP : at + rows] = mine[:, src + HALF : src + HALF + rows - TOP]


def analysis_kernel(x_ref, lh_ref, ll_ref, out_ref, ct, tmp):
    for k in range(4):
        tmp[:, k * 128 : (k + 1) * 128] = x_ref[:, k, :]
    for a in range(8):
        for r in range(2):
            for j in range(5):
                q = (r * 5 + j) * 16
                lane = r * 256 + j * WIDE
                ct[q : q + 16, a * WIDE : (a + 1) * WIDE] = tmp[a * 16 : a * 16 + 16, lane : lane + WIDE]
    ch, cl = two(ct[...])
    n = ch.shape[0]
    both = dot(jnp.concatenate([ch, cl], axis=0), lh_ref[...], NN)
    out_ref[...] = both[:n] + both[n:] + dot(ch, ll_ref[...], NN)


def synthesis_kernel(place_ref, near_ref, far_ref, lh_ref, ll_ref, sv_ref, w_ref, out_ref, back):
    half, degrees = w_ref.shape[0] // 2, w_ref.shape[1]
    n, rows = 2 * half, degrees // 16
    back[...] = jnp.zeros_like(back)
    spec = near_ref[...] + far_ref[...]
    g, h = spec[:half], spec[half:]
    u, v = w_ref[:half, :], w_ref[half:, :]
    twice = jnp.where(place_ref[2] == 1, 1.0, 2.0).astype(F32)
    adjoint = jnp.concatenate([(u * g + v * h) * twice, (u * h - v * g) * twice], axis=0)
    p, q = sv_ref[:half, :], sv_ref[half:, :]
    own = jnp.where(place_ref[1] == 0, spec[:, : degrees // 2], spec[:, degrees // 2 :])
    g, h = own[:half], own[half:]
    part = (p * g + q * h, p * h - q * g)
    ah, al = two(adjoint)
    both = dot(jnp.concatenate([ah, al], axis=0), lh_ref[...], NT)
    syn = both[:n] + both[n:] + dot(ah, ll_ref[...], NT)
    for a in range(8):
        to = slice(a * 16, a * 16 + 16)
        for r in range(2):
            for j in range(5):
                at = (r * 5 + j) * 16
                lane = r * 256 + j * WIDE
                back[to, lane : lane + WIDE] = syn[at : at + 16, a * WIDE : (a + 1) * WIDE]
                piece = part[r][j * 16 : j * 16 + 16, a * rows : (a + 1) * rows]
                back[to, 512 + lane : 512 + lane + rows] = piece
    for k in range(8):
        out_ref[:, k, :] = back[:, k * 128 : (k + 1) * 128]


def share_kernel(x_ref, out_ref):
    total = jnp.sum(x_ref[...], axis=0)[4:8]
    out_ref[...] = jnp.broadcast_to(total[None], out_ref.shape)


def inverse_kernel(x_ref, th_ref, tl_ref, lw_ref, out_ref):
    group, rows, points = out_ref.shape
    block = jnp.concatenate(
        [jnp.concatenate([x_ref[:, 2 * r, :], x_ref[:, 2 * r + 1, :]], axis=1) for r in range(2)], axis=0
    )
    high, low = two(block)
    table = th_ref[...]
    acc = dot(high, table, TN) + dot(low, table, TN) + dot(high, tl_ref[...], TN)
    for j in range(group):
        at = j * WIDE
        out_ref[j, :TOP, :] = acc[at : at + TOP] * lw_ref[:TOP, :]
        out_ref[j, TOP:, :] = acc[at + HALF : at + HALF + rows - TOP] * lw_ref[TOP:, :]


def call(kernel, args, out_shapes, flops, scratch=(), scalars=0, hbm_out=False):
    vmem = pl.BlockSpec(memory_space=pltpu.VMEM)
    smem = pl.BlockSpec(memory_space=pltpu.SMEM)
    moved = sum(a.size * a.dtype.itemsize for a in (*args, *jax.tree.leaves(out_shapes)))
    extra = {} if hbm_out else dict(out_specs=jax.tree.map(lambda s: vmem, out_shapes))
    return pl.pallas_call(
        kernel,
        out_shape=out_shapes,
        in_specs=[smem if i < scalars else vmem for i in range(len(args))],
        scratch_shapes=list(scratch),
        compiler_params=pltpu.CompilerParams(vmem_limit_bytes=24 * 2**20),
        cost_estimate=pl.CostEstimate(flops=flops, bytes_accessed=moved, transcendentals=0),
        **extra,
    )(*args)


def shape(*dims, dtype=F32):
    return jax.ShapeDtypeStruct(dims, dtype)


def local(grad_out, saved_spectra, spec_weight, legendre, lat_weight):
    group, rows, points = grad_out.shape
    degrees, _, channels = spec_weight.shape
    orders = legendre.shape[0]
    half = channels // 2
    yh, z, yl, x, c = (lax.axis_index(n) for n in NAMES)
    first = z + yl + x == 0
    place = jnp.stack([c, yh, first.astype(jnp.int32)]).astype(jnp.int32)
    slot_table = jnp.asarray(channel_slots(channels))
    slots = jnp.where(c == 0, slot_table[0:1], slot_table[1:2])
    high, low = (jnp.asarray(t) for t in tables(points))

    rows_out = call(
        prepare_kernel,
        (legendre, saved_spectra),
        shape(2, orders + 1, HALF, 8 * 128),
        1000,
    )
    rows_out = lax.all_to_all(rows_out, ("c",), 0, 0, tiled=True)
    near = lax.all_to_all(rows_out.reshape(8, HALF, -1), ("z",), 0, 0, tiled=True)

    coeffs = call(
        forward_kernel,
        (grad_out, high, low),
        shape(128, 4, 128),
        600_000_000,
        scratch=[pltpu.VMEM((256, points), F32)],
    )
    coeffs, near = lax.optimization_barrier((coeffs, near))
    far = lax.ppermute(near, ("c",), [(0, 1), (1, 0)])
    coeffs = lax.all_to_all(coeffs, GROUP, 0, 0, tiled=True)
    leg_high, leg_low, sv = call(
        split_kernel,
        (place, slots, near, far),
        (
            shape(8 * WIDE, degrees, dtype=BF),
            shape(8 * WIDE, degrees, dtype=BF),
            shape(2 * half, degrees // 2),
        ),
        100_000_000,
        scratch=[pltpu.VMEM((8, WIDE, 8 * 128), F32), pltpu.VMEM((8, WIDE, channels), F32)],
        scalars=1,
    )
    spectra = call(
        analysis_kernel,
        (coeffs, leg_high, leg_low),
        shape(2 * half, degrees),
        300_000_000,
        scratch=[pltpu.VMEM((2 * half, 8 * WIDE), F32), pltpu.VMEM((128, 512), F32)],
    )
    spectra, spec_weight = lax.optimization_barrier((spectra, spec_weight))
    weight = call(weight_kernel, (slots, spec_weight.transpose(1, 2, 0)), shape(2 * half, degrees), 100_000_000)
    other = lax.ppermute(spectra, ("yh",), [(0, 1), (1, 0)])
    back = call(
        synthesis_kernel,
        (place, spectra, other, leg_high, leg_low, sv, weight),
        shape(128, 8, 128),
        300_000_000,
        scratch=[pltpu.VMEM((128, 1024), F32)],
        scalars=1,
    )
    back = lax.all_to_all(back, GROUP, 0, 0, tiled=True)

    share = call(share_kernel, (back,), shape(32, 4, 128), 1_000_000)
    share = lax.all_to_all(share, LON, 0, 0, tiled=True)
    grad_in = call(
        inverse_kernel,
        (back, high, low, lat_weight.reshape(rows, 1)),
        shape(group, rows, points),
        600_000_000,
        hbm_out=True,
    )
    grad_weight = share.reshape(32, 2, 256)[..., : group * WIDE].reshape(32, 2, group, WIDE)[..., :rows]
    grad_weight = grad_weight.transpose(3, 1, 0, 2).reshape(rows, 2, channels)
    return (grad_in, grad_weight)


def solution(mesh):
    fine = Mesh(mesh.devices.reshape(SIZES), NAMES)
    return jax.shard_map(
        local,
        mesh=fine,
        in_specs=(P(LON, LAT, None), P(LAT, LON, None, None), P(), P(LON, LAT, None), P(LAT)),
        out_specs=(P(LON, LAT, None), P(LAT, None, None)),
        check_vma=False,
    )
```

```python
import functools
import math

import jax
import jax.numpy as jnp
import ml_dtypes
import numpy as np
from jax import lax
from jax.experimental import pallas as pl
from jax.experimental.pallas import tpu as pltpu
from jax.sharding import Mesh, PartitionSpec as P

NAMES = ("yh", "z", "yl", "x", "c")
SIZES = (2, 8, 4, 4, 2)
LAT = ("yh", "z")
LON = ("yl", "x", "c")
GROUP = ("z", "yl", "x")
BF = jnp.bfloat16
F32 = jnp.float32
WIDE = 48
HALF = WIDE // 2
TOP = HALF - 1
PICK = (((0,), (1,)), ((), ()))
NN = (((1,), (0,)), ((), ()))
NT = (((1,), (1,)), ((), ()))
TN = (((0,), (0,)), ((), ()))


@functools.cache
def tables(points):
    z, yl, x = (n.reshape(-1) for n in np.meshgrid(*map(np.arange, (8, 4, 4)), indexing="ij"))
    m = 3 * ((yl * 4 + x) * 2 + z // 4) + z % 4
    phase = (m[:, None] * np.arange(points)[None]) % points
    angle = 2.0 * math.pi / points * phase
    rows = np.stack([np.cos(angle), -np.sin(angle)]) / math.sqrt(points)
    full = np.where(z[None, :, None] % 4 < 3, rows, 0.0).reshape(256, points).astype(np.float32)
    high = full.astype(ml_dtypes.bfloat16)
    low = (full - high.astype(np.float32)).astype(ml_dtypes.bfloat16)
    return high, low


def channel_slots(channels):
    per = channels // 32
    c, j, b = np.meshgrid(np.arange(2), np.arange(per), np.arange(16), indexing="ij")
    return ((b * 2 + c) * per + j).reshape(2, channels // 2).astype(np.int32)


def dot(a, b, dims):
    return lax.dot_general(a, b, dims, preferred_element_type=F32)


def two(x):
    high = x.astype(BF)
    return high, (x - high.astype(F32)).astype(BF)


def three(x):
    high, rest = x.astype(BF), None
    rest = x - high.astype(F32)
    mid = rest.astype(BF)
    return high, mid, (rest - mid.astype(F32)).astype(BF)


def prepare_kernel(leg_ref, saved_ref, out_ref):
    orders, rows, degrees = leg_ref.shape
    channels = saved_ref.shape[3]
    lanes = out_ref.shape[3]
    fit = lanes - degrees - channels
    rest = channels - fit
    out_ref[...] = jnp.zeros_like(out_ref)
    for side, (low, n) in enumerate(((0, TOP), (TOP, rows - TOP))):
        at = slice(low, low + n)
        for k in range(orders):
            out_ref[side, k, :n, :degrees] = leg_ref[k, at, :]
            out_ref[side, k, :n, degrees : degrees + channels] = saved_ref[at, k, 0, :]
            out_ref[side, k, :n, degrees + channels :] = saved_ref[at, k, 1, :fit]
            for i in range(n):
                tail = saved_ref[low + i : low + i + 1, k, 1, fit:]
                out_ref[side, k, TOP:HALF, i * rest : (i + 1) * rest] = tail


def picks(slots_ref, channels):
    n = slots_ref.shape[1]
    return (lax.broadcasted_iota(jnp.int32, (channels, n), 0) == slots_ref[...]).astype(F32).astype(BF)


def weight_kernel(slots_ref, w_ref, out_ref):
    _, channels, _ = w_ref.shape
    half = channels // 2
    pick = picks(slots_ref, channels)
    for r in range(2):
        out_ref[r * half : (r + 1) * half, :] = sum(dot(pick, term, TN) for term in three(w_ref[r]))


def forward_kernel(g_ref, th_ref, tl_ref, out_ref, field):
    group, rows, points = g_ref.shape
    field[...] = jnp.zeros_like(field)
    for j in range(group):
        field[j * WIDE : j * WIDE + TOP, :] = g_ref[j, :TOP, :]
        field[j * WIDE + HALF : j * WIDE + HALF + rows - TOP, :] = g_ref[j, TOP:, :]
    high, low = two(field[...])
    table = th_ref[...]
    acc = dot(table, high, NT) + dot(table, low, NT) + dot(tl_ref[...], high, NT)
    for r in range(2):
        for k in range(2):
            out_ref[:, 2 * r + k, :] = acc[r * 128 : (r + 1) * 128, k * 128 : (k + 1) * 128]


def split_kernel(place_ref, slots_ref, near_ref, far_ref, lh_ref, ll_ref, sv_ref, both, second):
    degrees = lh_ref.shape[1]
    half = sv_ref.shape[0] // 2
    channels = 2 * half
    rows = degrees // 16
    fit = both.shape[2] - degrees - channels
    rest = channels - fit
    c = place_ref[0]
    both[:, pl.ds(pl.multiple_of(c * HALF, HALF), HALF), :] = near_ref[...]
    both[:, pl.ds(pl.multiple_of((1 - c) * HALF, HALF), HALF), :] = far_ref[...]
    high, low = two(both[:, :, :degrees].reshape(8 * WIDE, degrees))
    lh_ref[...] = high
    ll_ref[...] = low
    second[...] = jnp.zeros_like(second)
    second[:, :, :fit] = both[:, :, degrees + channels :]
    for side, n in enumerate((TOP, rows - TOP)):
        for i in range(n):
            second[:, side * HALF + i, fit:] = both[:, side * HALF + TOP, i * rest : (i + 1) * rest]
    pick = picks(slots_ref, channels)
    for r, v in enumerate((both[:, :, degrees : degrees + channels], second[...])):
        mine = sum(dot(pick, term, PICK) for term in three(v.reshape(8 * WIDE, channels)))
        to = slice(r * half, (r + 1) * half)
        for a in range(8):
            at, src = a * rows, a * WIDE
            sv_ref[to, at : at + TOP] = mine[:, src : src + TOP]
            sv_ref[to, at + TOP : at + rows] = mine[:, src + HALF : src + HALF + rows - TOP]


def moves(half):
    at = 5 * 2 * half
    out = [(slice(0, half), slice(640, 720), slice(at, at + half), slice(0, 80))]
    out.append((slice(half, 2 * half), slice(640, 688), slice(at, at + half), slice(80, 128)))
    for i, low in enumerate(range(0, half, 24)):
        n = min(24, half - low)
        rows = slice(half + low, half + low + n)
        out.append((rows, slice(688, 720), slice(at + half, at + half + n), slice(32 * i, 32 * i + 32)))
    for k in range(5):
        out.append((slice(0, 2 * half), slice(128 * k, 128 * k + 128), slice(2 * half * k, 2 * half * (k + 1)), slice(0, 128)))
    return out


def analysis_kernel(x_ref, lh_ref, ll_ref, out_ref, ct, tmp):
    for k in range(4):
        tmp[:, k * 128 : (k + 1) * 128] = x_ref[:, k, :]
    for a in range(8):
        for r in range(2):
            for j in range(5):
                q = (r * 5 + j) * 16
                lane = r * 256 + j * WIDE
                ct[q : q + 16, a * WIDE : (a + 1) * WIDE] = tmp[a * 16 : a * 16 + 16, lane : lane + WIDE]
    ch, cl = two(ct[...])
    n = ch.shape[0]
    both = dot(jnp.concatenate([ch, cl], axis=0), lh_ref[...], NN)
    spec = both[:n] + both[n:] + dot(ch, ll_ref[...], NN)
    out_ref[out_ref.shape[0] - 24 :, :] = jnp.zeros((24, 128), F32)
    for rows, lanes, to, there in moves(n // 2):
        out_ref[to, there] = spec[rows, lanes]


def synthesis_kernel(place_ref, near_ref, far_ref, lh_ref, ll_ref, sv_ref, w_ref, out_ref, back, full):
    half, degrees = w_ref.shape[0] // 2, w_ref.shape[1]
    n, rows = 2 * half, degrees // 16
    back[...] = jnp.zeros_like(back)
    for to, there, at, lanes in moves(half):
        full[to, there] = near_ref[at, lanes] + far_ref[at, lanes]
    spec = full[...]
    g, h = spec[:half], spec[half:]
    u, v = w_ref[:half, :], w_ref[half:, :]
    twice = jnp.where(place_ref[2] == 1, 1.0, 2.0).astype(F32)
    adjoint = jnp.concatenate([(u * g + v * h) * twice, (u * h - v * g) * twice], axis=0)
    p, q = sv_ref[:half, :], sv_ref[half:, :]
    own = jnp.where(place_ref[1] == 0, spec[:, : degrees // 2], spec[:, degrees // 2 :])
    g, h = own[:half], own[half:]
    part = (p * g + q * h, p * h - q * g)
    ah, al = two(adjoint)
    both = dot(jnp.concatenate([ah, al], axis=0), lh_ref[...], NT)
    syn = both[:n] + both[n:] + dot(ah, ll_ref[...], NT)
    for a in range(8):
        to = slice(a * 16, a * 16 + 16)
        for r in range(2):
            for j in range(5):
                at = (r * 5 + j) * 16
                lane = r * 256 + j * WIDE
                back[to, lane : lane + WIDE] = syn[at : at + 16, a * WIDE : (a + 1) * WIDE]
                piece = part[r][j * 16 : j * 16 + 16, a * rows : (a + 1) * rows]
                back[to, 512 + lane : 512 + lane + rows] = piece
    for k in range(8):
        out_ref[:, k, :] = back[:, k * 128 : (k + 1) * 128]


def share_kernel(x_ref, out_ref):
    total = jnp.sum(x_ref[...], axis=0)[4:8]
    out_ref[...] = jnp.broadcast_to(total[None], out_ref.shape)


def inverse_kernel(x_ref, th_ref, tl_ref, lw_ref, out_ref):
    group, rows, points = out_ref.shape
    block = jnp.concatenate(
        [jnp.concatenate([x_ref[:, 2 * r, :], x_ref[:, 2 * r + 1, :]], axis=1) for r in range(2)], axis=0
    )
    high, low = two(block)
    table = th_ref[...]
    acc = dot(high, table, TN) + dot(low, table, TN) + dot(high, tl_ref[...], TN)
    for j in range(group):
        at = j * WIDE
        out_ref[j, :TOP, :] = acc[at : at + TOP] * lw_ref[:TOP, :]
        out_ref[j, TOP:, :] = acc[at + HALF : at + HALF + rows - TOP] * lw_ref[TOP:, :]


def call(kernel, args, out_shapes, flops, scratch=(), scalars=0, hbm_out=False):
    vmem = pl.BlockSpec(memory_space=pltpu.VMEM)
    smem = pl.BlockSpec(memory_space=pltpu.SMEM)
    moved = sum(a.size * a.dtype.itemsize for a in (*args, *jax.tree.leaves(out_shapes)))
    extra = {} if hbm_out else dict(out_specs=jax.tree.map(lambda s: vmem, out_shapes))
    return pl.pallas_call(
        kernel,
        out_shape=out_shapes,
        in_specs=[smem if i < scalars else vmem for i in range(len(args))],
        scratch_shapes=list(scratch),
        compiler_params=pltpu.CompilerParams(vmem_limit_bytes=24 * 2**20),
        cost_estimate=pl.CostEstimate(flops=flops, bytes_accessed=moved, transcendentals=0),
        **extra,
    )(*args)


def shape(*dims, dtype=F32):
    return jax.ShapeDtypeStruct(dims, dtype)


def local(grad_out, saved_spectra, spec_weight, legendre, lat_weight):
    group, rows, points = grad_out.shape
    degrees, _, channels = spec_weight.shape
    orders = legendre.shape[0]
    half = channels // 2
    yh, z, yl, x, c = (lax.axis_index(n) for n in NAMES)
    first = z + yl + x == 0
    place = jnp.stack([c, yh, first.astype(jnp.int32)]).astype(jnp.int32)
    slot_table = jnp.asarray(channel_slots(channels))
    slots = jnp.where(c == 0, slot_table[0:1], slot_table[1:2])
    high, low = (jnp.asarray(t) for t in tables(points))

    rows_out = call(
        prepare_kernel,
        (legendre, saved_spectra),
        shape(2, orders + 1, HALF, 8 * 128),
        1000,
    )
    rows_out = lax.all_to_all(rows_out, ("c",), 0, 0, tiled=True)
    near = lax.all_to_all(rows_out.reshape(8, HALF, -1), ("z",), 0, 0, tiled=True)

    coeffs = call(
        forward_kernel,
        (grad_out, high, low),
        shape(128, 4, 128),
        600_000_000,
        scratch=[pltpu.VMEM((256, points), F32)],
    )
    coeffs, near = lax.optimization_barrier((coeffs, near))
    far = lax.ppermute(near, ("c",), [(0, 1), (1, 0)])
    coeffs = lax.all_to_all(coeffs, GROUP, 0, 0, tiled=True)
    leg_high, leg_low, sv = call(
        split_kernel,
        (place, slots, near, far),
        (
            shape(8 * WIDE, degrees, dtype=BF),
            shape(8 * WIDE, degrees, dtype=BF),
            shape(2 * half, degrees // 2),
        ),
        100_000_000,
        scratch=[pltpu.VMEM((8, WIDE, 8 * 128), F32), pltpu.VMEM((8, WIDE, channels), F32)],
        scalars=1,
    )
    spectra = call(
        analysis_kernel,
        (coeffs, leg_high, leg_low),
        shape(11 * half + 24, 128),
        300_000_000,
        scratch=[pltpu.VMEM((2 * half, 8 * WIDE), F32), pltpu.VMEM((128, 512), F32)],
    )
    spectra, spec_weight = lax.optimization_barrier((spectra, spec_weight))
    weight = call(weight_kernel, (slots, spec_weight.transpose(1, 2, 0)), shape(2 * half, degrees), 100_000_000)
    other = lax.ppermute(spectra, ("yh",), [(0, 1), (1, 0)])
    back = call(
        synthesis_kernel,
        (place, spectra, other, leg_high, leg_low, sv, weight),
        shape(128, 8, 128),
        300_000_000,
        scratch=[pltpu.VMEM((128, 1024), F32), pltpu.VMEM((2 * half, degrees), F32)],
        scalars=1,
    )
    back = lax.all_to_all(back, GROUP, 0, 0, tiled=True)

    share = call(share_kernel, (back,), shape(32, 4, 128), 1_000_000)
    share = lax.all_to_all(share, LON, 0, 0, tiled=True)
    grad_in = call(
        inverse_kernel,
        (back, high, low, lat_weight.reshape(rows, 1)),
        shape(group, rows, points),
        600_000_000,
        hbm_out=True,
    )
    grad_weight = share.reshape(32, 2, 256)[..., : group * WIDE].reshape(32, 2, group, WIDE)[..., :rows]
    grad_weight = grad_weight.transpose(3, 1, 0, 2).reshape(rows, 2, channels)
    return (grad_in, grad_weight)


def solution(mesh):
    fine = Mesh(mesh.devices.reshape(SIZES), NAMES)
    return jax.shard_map(
        local,
        mesh=fine,
        in_specs=(P(LON, LAT, None), P(LAT, LON, None, None), P(), P(LON, LAT, None), P(LAT)),
        out_specs=(P(LON, LAT, None), P(LAT, None, None)),
        check_vma=False,
    )
```
